512 devices in a mesh: island: 8 (over z_lo, x), replica: 8 (over z_hi, core), shard: 8 (over y).
Axes of the slice: x: 4, y: 8, z: 8 (z_hi: 4, z_lo: 2; z = z_hi * 2 + z_lo), core: 2. Of those that a mesh axis runs over, the one named last changes fastest.
Arguments:
- inputs: bfloat16 [2, 131072, 4096], P(None, ('island', 'replica', 'shard')), may hold values from -24 to 24
- targets: bfloat16 [2, 131072, 128], P(None, ('island', 'replica', 'shard')), may hold values from -6 to 6
- theta: float32 [4096, 128], P(('replica', 'shard')), may hold values from -6 to 6
- momentum: float32 [4096, 128], P(('replica', 'shard')), may hold values from -0.6 to 0.6
- first_moment: float32 [8, 4096, 128], P('island', ('replica', 'shard')), may hold values from -2 to 2
- second_moment: float32 [8, 4096, 128], P('island', ('replica', 'shard')), may hold values from 0.001 to 1
Outputs:
- theta_new: float32 [4096, 128], P(('replica', 'shard'))
- momentum_new: float32 [4096, 128], P(('replica', 'shard'))
- first_out: float32 [8, 4096, 128], P('island', ('replica', 'shard'))
- second_out: float32 [8, 4096, 128], P('island', ('replica', 'shard'))
The draws below stay inside these ranges and needn't reach their ends.
All inputs are finite; a program needn't handle non-finite values.
Results may differ from the reference program's by a relative error of at most 0.0051.
Values may be sent and summed in bfloat16 or wider, within the bound.
A program may use at most 64 MiB of HBM per device.

```python
import math
import jax
import jax.numpy as jnp
from jax import lax

D = 4096
HEAD = 128
INNER = 2
ISLANDS = 8
TOKENS = 131072


def raised(drawn, key, source, target, parts, factor):
    def block_of(dim):
        return (jnp.arange(drawn.shape[dim]) // (drawn.shape[dim] // parts)).reshape((-1,) + (1,) * (drawn.ndim - 1 - dim))

    one_side = jax.random.permutation(key, parts)[block_of(target)]
    other_side = (block_of(target) + parts // 2) % parts
    return jnp.where((block_of(source) == one_side) | (block_of(source) == other_side), factor * drawn, drawn)


def levels(stream_key, extent, cuts, smallest, top_value):
    def one(dim, blocks):
        heights = jax.random.uniform(jax.random.fold_in(jax.random.fold_in(stream_key, 6), dim), (blocks,), jnp.float32, smallest / len(cuts), top_value / len(cuts))
        return jnp.repeat(jnp.exp(heights), extent[dim] // blocks).reshape((-1,) + (1,) * (len(extent) - dim - 1))

    level = one(*cuts[0])
    for cut in cuts[1:]:
        level = level * one(*cut)
    return level


def bell_draw(own_key, extent, scale, bound, pieces=(), held_as=jnp.bfloat16):
    values = jax.random.normal(own_key, extent, jnp.float32) * scale
    if len(pieces) > 0:
        values = levels(own_key, extent, pieces, -0.22, 0.18) * values
    return jnp.clip(values, min=-bound, max=bound).astype(held_as)


def noise_with(rng, dims, width, reach, shards, heavy, dtype=jnp.bfloat16):
    entries = width * jax.random.normal(rng, dims, jnp.float32)
    if shards:
        entries = entries * levels(rng, dims, shards, -0.22, 0.18)
    return jnp.clip(raised(entries, jax.random.fold_in(rng, 3), *heavy), -reach, reach).astype(dtype)


def setup_inputs(seed: int = 0) -> dict:
    key_of = jax.random.split(jax.random.key(seed), 7)
    return {
        "inputs": noise_with(key_of[0], (INNER, TOKENS, D), 1.0, 24.0, ((1, 512),), (1, 2, 512, 6.0)),
        "targets": bell_draw(key_of[1], (INNER, TOKENS, HEAD), 1.0, 6.0, ((1, 512),)),
        "theta": bell_draw(key_of[2], (D, HEAD), 1.0, 6.0, ((0, 64),), jnp.float32),
        "momentum": bell_draw(key_of[3], (D, HEAD), 0.1, 0.6, ((0, 64),), jnp.float32),
        "first_moment": bell_draw(key_of[4], (ISLANDS, D, HEAD), 0.3, 2.0, ((0, 8), (1, 64)), jnp.float32),
        "second_moment": jnp.clip(jnp.exp(math.log(1.0) - 6.9077552 * jax.random.uniform(key_of[5], (ISLANDS, D, HEAD), jnp.float32) ** levels(key_of[5], (ISLANDS, D, HEAD), ((0, 8), (1, 64)), -0.2, 0.2)), 0.001, 1.0),
    }


BETA_ONE = 0.9
BETA_TWO = 0.95
EPSILON = 1e-08
INNER_RATE = 0.05
DECAY = 0.1
OUTER_RATE = 0.7
OUTER_MOMENTUM = 0.9

def reference(inputs, targets, theta, momentum, first_moment, second_moment):
    island_count = first_moment.shape[0]
    island_tokens = inputs.shape[1] // island_count
    key_scale = D ** (-0.5)
    grad_scale = 1.0 / math.sqrt(island_tokens)
    summed = jnp.zeros_like(theta)
    first_list = []
    second_list = []
    for island in range(island_count):
        parameters = theta
        first = first_moment[island]
        second = second_moment[island]
        for inner_step in range(INNER):
            batch_inputs = inputs[inner_step, island * island_tokens:(island + 1) * island_tokens]
            batch_targets = targets[inner_step, island * island_tokens:(island + 1) * island_tokens]
            weights_half = parameters.astype(jnp.bfloat16)
            projected = jnp.dot(batch_inputs, weights_half, preferred_element_type=jnp.float32) * key_scale
            residual = (projected - batch_targets.astype(jnp.float32)).astype(jnp.bfloat16)
            gradient = lax.dot_general(batch_inputs, residual, (((0,), (0,)), ((), ())), preferred_element_type=jnp.float32) * grad_scale
            first = BETA_ONE * first + (1.0 - BETA_ONE) * gradient
            second = BETA_TWO * second + (1.0 - BETA_TWO) * gradient * gradient
            parameters = parameters - INNER_RATE * (first / (jnp.sqrt(second) + EPSILON) + DECAY * parameters)
        summed = summed + parameters
        first_list.append(first)
        second_list.append(second)
    mean_params = summed / island_count
    pseudo_grad = theta - mean_params
    momentum_new = OUTER_MOMENTUM * momentum + pseudo_grad
    theta_new = theta - OUTER_RATE * (pseudo_grad + OUTER_MOMENTUM * momentum_new)
    return (theta_new, momentum_new, jnp.stack(first_list), jnp.stack(second_list))
```

```python
import functools
import math

import jax
import jax.numpy as jnp
from jax import lax
from jax.experimental import pallas as pl
from jax.experimental.pallas import tpu as pltpu
from jax.sharding import PartitionSpec as P

BETA_ONE = 0.9
BETA_TWO = 0.95
EPSILON = 1e-08
INNER_RATE = 0.05
DECAY = 0.1
OUTER_RATE = 0.7
OUTER_MOMENTUM = 0.9

MESH = pl.DeviceIdType.MESH
F32 = jnp.float32
BF16 = jnp.bfloat16


def kernel(
    sizes,
    x_hbm, t_hbm, theta_hbm, momentum_hbm, first_hbm, second_hbm,
    theta_out, momentum_out, first_out, second_out,
    xs, xt, ts, state, weights, part_out, part_in,
    grads, near_a, sum_a, far_a, near_b, sum_b, far_b,
    pool_out, pool_in,
    x_local, x_send, x_recv, t_sems, state_sems, out_sems,
    part_send, part_recv, send, recv, pool_send, pool_recv,
):
    steps, depths, rows, islands = sizes
    island = lax.axis_index("island")
    replica = lax.axis_index("replica")
    row = lax.axis_index("shard")
    depth, core = replica // 2, replica % 2
    tokens = x_hbm.shape[1]
    width = xs.shape[3]
    head = t_hbm.shape[2]
    half = weights.shape[4]
    key_scale = (depths * 2 * width) ** (-0.5)
    grad_scale = 1.0 / math.sqrt(tokens * 2 * depths * rows)

    def over_rows(offset):
        return {"shard": (row + offset) % rows}

    def over_depths(offset):
        return {"replica": (depth + offset) % depths * 2 + core}

    sibling = {"replica": depth * 2 + 1 - core}

    def over_islands(offset):
        return {"island": (island + offset) % islands}

    def remote(source, target, send_sem, recv_sem, where):
        return pltpu.make_async_remote_copy(
            src_ref=source, dst_ref=target, send_sem=send_sem, recv_sem=recv_sem,
            device_id=where, device_id_type=MESH,
        )

    barrier = pltpu.get_barrier_semaphore()
    greeted = [over_rows(k) for k in range(1, rows)] + [over_depths(k) for k in range(1, depths)]
    greeted += [sibling] + [over_islands(k) for k in range(1, islands)]
    for where in greeted:
        pl.semaphore_signal(barrier, inc=1, device_id=where, device_id_type=MESH)

    def load(k, source):
        return pltpu.make_async_copy(source, state.at[k], state_sems.at[k])

    loads = [load(0, theta_hbm), load(1, momentum_hbm), load(2, first_hbm), load(3, second_hbm)]
    loads[0].start()
    own_tokens = pl.ds(pl.multiple_of(core * tokens, tokens), tokens)

    def x_columns(z, which):
        return pl.ds(pl.multiple_of((z * 2 + which) * width, width), width)

    def x_mine(s, z):
        return pltpu.make_async_copy(
            x_hbm.at[s, :, x_columns(z, core)], xs.at[s, z, own_tokens], x_local.at[s, z]
        )

    def x_theirs(s, z):
        return remote(
            x_hbm.at[s, :, x_columns(z, 1 - core)], xs.at[s, z, own_tokens],
            x_send.at[s, z], x_recv.at[s, z], sibling,
        )

    t_mine = pltpu.make_async_copy(t_hbm, ts.at[:, own_tokens], t_sems.at[0])
    t_theirs = remote(t_hbm, ts.at[:, own_tokens], t_sems.at[1], t_sems.at[2], sibling)
    for z in range(depths):
        x_mine(0, z).start()
    t_mine.start()
    for k in (1, 2, 3):
        loads[k].start()
    for s in range(1, steps):
        for z in range(depths):
            x_mine(s, z).start()

    def gather_near_a(s, k):
        block = weights.at[s, depth, row, 0]
        return remote(block, block, send.at[s, 0, k - 1], recv.at[s, 0, k - 1], over_rows(k))

    def gather_near_b(s, k):
        block, i = weights.at[s, depth, row, 1], rows + k - 2
        return remote(block, block, send.at[s, 0, i], recv.at[s, 0, i], over_depths(k))

    def gather_far_a(s, k):
        block, i = weights.at[s, depth, :, 0], rows + depths + k - 3
        return remote(block, block, send.at[s, 0, i], recv.at[s, 0, i], over_depths(k))

    def gather_far_b(s, k):
        block, i = weights.at[s, :, row, 1], rows + 2 * depths + k - 4
        return remote(block, block, send.at[s, 0, i], recv.at[s, 0, i], over_rows(k))

    def scatter_near_a(s, k):
        block, i = grads.at[s, (depth + k) % depths, :, 0], k - 1
        return remote(block, near_a.at[s, k - 1], send.at[s, 1, i], recv.at[s, 1, i], over_depths(k))

    def scatter_near_b(s, k):
        block, i = grads.at[s, :, (row + k) % rows, 1], depths + k - 2
        return remote(block, near_b.at[s, k - 1], send.at[s, 1, i], recv.at[s, 1, i], over_rows(k))

    def scatter_far_a(s, k):
        block, i = sum_a.at[s, (row + k) % rows], depths + rows + k - 3
        return remote(block, far_a.at[s, k - 1], send.at[s, 1, i], recv.at[s, 1, i], over_rows(k))

    def scatter_far_b(s, k):
        block, i = sum_b.at[s, (depth + k) % depths], depths + 2 * rows + k - 4
        return remote(block, far_b.at[s, k - 1], send.at[s, 1, i], recv.at[s, 1, i], over_depths(k))

    def over(copies_of, s, count):
        return [copies_of(s, k) for k in range(1, count)]

    def start(copies):
        for copy in copies:
            copy.start()

    def arrive(copies):
        for copy in copies:
            copy.wait_recv()

    def transposed(s):
        for z in range(depths):
            xt[s, z] = xs[s, z].T

    loads[0].wait()
    weights[0, depth, row] = state[0].astype(BF16)
    pl.semaphore_wait(barrier, len(greeted))

    for s in range(steps):
        start(over(gather_near_b, s, depths) + over(gather_near_a, s, rows))
        if s == 0:
            for z in range(depths):
                x_theirs(0, z).start()
            t_theirs.start()
        arrive(over(gather_near_b, s, depths))
        start(over(gather_far_b, s, rows))
        arrive(over(gather_near_a, s, rows))
        start(over(gather_far_a, s, depths))
        if s == 0:
            for later in range(1, steps):
                for z in range(depths):
                    x_theirs(later, z).start()
            t_mine.wait()
            t_theirs.wait_recv()
        for z in range(depths):
            x_mine(s, z).wait()
            x_theirs(s, z).wait_recv()
        transposed(s)
        arrive(over(gather_far_b, s, rows) + over(gather_far_a, s, depths))

        def part(p):
            block = part_out.at[s, pl.ds(p * tokens, tokens)]
            return remote(
                block, part_in.at[s, pl.ds(p * tokens, tokens)],
                part_send.at[s, p], part_recv.at[s, p], sibling,
            )

        for p in range(2):
            total = jnp.zeros((tokens, head), F32)
            for z in range(depths):
                total += jnp.dot(
                    xs[s, z, p * tokens:(p + 1) * tokens],
                    weights[s, z].reshape(width, head),
                    preferred_element_type=F32,
                )
            part_out[s, p * tokens:(p + 1) * tokens] = total
            part(p).start()
        arrive([part(0), part(1)])
        projected = (part_out[s] + part_in[s]) * key_scale
        residual = (projected - ts[s].astype(F32)).astype(BF16)

        for z in range(depths):
            gradient = jnp.dot(xt[s, z], residual, preferred_element_type=F32) * grad_scale
            grads[s, z] = gradient.astype(BF16).reshape(rows, 2, half, head)
        start(over(scatter_near_a, s, depths) + over(scatter_near_b, s, rows))
        arrive(over(scatter_near_a, s, depths))
        total_a = grads[s, depth, :, 0].astype(F32)
        for k in range(depths - 1):
            total_a += near_a[s, k].astype(F32)
        sum_a[s] = total_a.astype(BF16)
        start(over(scatter_far_a, s, rows))
        arrive(over(scatter_near_b, s, rows))
        total_b = grads[s, :, row, 1].astype(F32)
        for k in range(rows - 1):
            total_b += near_b[s, k].astype(F32)
        sum_b[s] = total_b.astype(BF16)
        start(over(scatter_far_b, s, depths))

        if s == 0:
            for k in (1, 2, 3):
                loads[k].wait()

        def update(part_index, gradient):
            parameters = state[0 if s == 0 else 4, part_index]
            first = BETA_ONE * state[2, part_index] + (1.0 - BETA_ONE) * gradient
            second = BETA_TWO * state[3, part_index] + (1.0 - BETA_TWO) * gradient * gradient
            parameters = parameters - INNER_RATE * (
                first / (jnp.sqrt(second) + EPSILON) + DECAY * parameters
            )
            state[2, part_index] = first
            state[3, part_index] = second
            state[4, part_index] = parameters
            if s < steps - 1:
                weights[s + 1, depth, row, part_index] = parameters.astype(BF16)

        arrive(over(scatter_far_a, s, rows))
        total_a = sum_a[s, row].astype(F32)
        for k in range(rows - 1):
            total_a += far_a[s, k].astype(F32)
        update(0, total_a)
        arrive(over(scatter_far_b, s, depths))
        total_b = sum_b[s, depth].astype(F32)
        for k in range(depths - 1):
            total_b += far_b[s, k].astype(F32)
        update(1, total_b)

    moved = state[0] - state[4]
    pool_out[...] = moved

    def pool(k):
        return remote(
            pool_out, pool_in.at[k - 1], pool_send.at[k - 1], pool_recv.at[k - 1], over_islands(k)
        )

    pools = [pool(k) for k in range(1, islands)]
    start(pools)
    stores = [
        pltpu.make_async_copy(state.at[2], first_out, out_sems.at[2]),
        pltpu.make_async_copy(state.at[3], second_out, out_sems.at[3]),
    ]
    start(stores)
    for z in range(depths):
        for s in range(steps):
            x_theirs(s, z).wait_send()
    t_theirs.wait_send()
    for s in range(steps):
        for p in range(2):
            block = part_out.at[s, pl.ds(p * tokens, tokens)]
            remote(block, block, part_send.at[s, p], part_recv.at[s, p], sibling).wait_send()
        for copies_of, count in (
            (gather_near_a, rows), (gather_near_b, depths), (gather_far_a, depths), (gather_far_b, rows),
            (scatter_near_a, depths), (scatter_near_b, rows), (scatter_far_a, rows), (scatter_far_b, depths),
        ):
            for copy in over(copies_of, s, count):
                copy.wait_send()
    arrive(pools)
    total = moved
    for k in range(islands - 1):
        total += pool_in[k]
    pseudo_grad = total / islands
    momentum_new = OUTER_MOMENTUM * state[1] + pseudo_grad
    state[1] = momentum_new
    state[4] = state[0] - OUTER_RATE * (pseudo_grad + OUTER_MOMENTUM * momentum_new)
    last = [
        pltpu.make_async_copy(state.at[4], theta_out, out_sems.at[0]),
        pltpu.make_async_copy(state.at[1], momentum_out, out_sems.at[1]),
    ]
    start(last)
    for copy in pools:
        copy.wait_send()
    for copy in stores + last:
        copy.wait()


def per_device(inputs, targets, theta, momentum, first_moment, second_moment):
    steps, tokens, _ = inputs.shape
    block, head = theta.shape
    islands = lax.axis_size("island")
    depths, rows = lax.axis_size("replica") // 2, lax.axis_size("shard")
    half, width = block // 2, rows * block
    split = (2, half, head)
    copies = 2 * (rows + depths - 2)
    dma = pltpu.SemaphoreType.DMA
    anywhere = pl.BlockSpec(memory_space=pl.ANY)
    vmem = pltpu.VMEM
    outs = pl.pallas_call(
        functools.partial(kernel, (steps, depths, rows, islands)),
        out_shape=[jax.ShapeDtypeStruct(split, F32)] * 4,
        in_specs=[anywhere] * 6,
        out_specs=[anywhere] * 4,
        scratch_shapes=[
            vmem((steps, depths, 2 * tokens, width), BF16),
            vmem((steps, depths, width, 2 * tokens), BF16),
            vmem((steps, 2 * tokens, head), BF16),
            vmem((5,) + split, F32),
            vmem((steps, depths, rows) + split, BF16),
            vmem((steps, 2 * tokens, head), F32),
            vmem((steps, 2 * tokens, head), F32),
            vmem((steps, depths, rows) + split, BF16),
            vmem((steps, depths - 1, rows, half, head), BF16),
            vmem((steps, rows, half, head), BF16),
            vmem((steps, rows - 1, half, head), BF16),
            vmem((steps, rows - 1, depths, half, head), BF16),
            vmem((steps, depths, half, head), BF16),
            vmem((steps, depths - 1, half, head), BF16),
            vmem(split, F32),
            vmem((islands - 1,) + split, F32),
            dma((steps, depths)), dma((steps, depths)), dma((steps, depths)),
            dma((3,)), dma((4,)), dma((4,)),
            dma((steps, 2)), dma((steps, 2)),
            dma((steps, 2, copies)), dma((steps, 2, copies)),
            dma((islands - 1,)), dma((islands - 1,)),
        ],
        compiler_params=pltpu.CompilerParams(
            collective_id=0, has_side_effects=True, vmem_limit_bytes=40 * 1024 * 1024
        ),
    )(
        inputs, targets, theta.reshape(split), momentum.reshape(split),
        first_moment.reshape(split), second_moment.reshape(split),
    )
    theta_new, momentum_new, first, second = [out.reshape(block, head) for out in outs]
    return (theta_new, momentum_new, first[None], second[None])


def solution(mesh):
    in_specs = (
        P(None, ("island", "replica", "shard"), None),
        P(None, ("island", "replica", "shard"), None),
        P(("replica", "shard"), None),
        P(("replica", "shard"), None),
        P("island", ("replica", "shard"), None),
        P("island", ("replica", "shard"), None),
    )
    out_specs = (
        P(("replica", "shard"), None),
        P(("replica", "shard"), None),
        P("island", ("replica", "shard"), None),
        P("island", ("replica", "shard"), None),
    )
    return jax.shard_map(
        per_device, mesh=mesh, in_specs=in_specs, out_specs=out_specs, check_vma=False
    )
```

```python
import functools
import math

import jax
import jax.numpy as jnp
from jax import lax
from jax.experimental import pallas as pl
from jax.experimental.pallas import tpu as pltpu
from jax.sharding import PartitionSpec as P

BETA_ONE = 0.9
BETA_TWO = 0.95
EPSILON = 1e-08
INNER_RATE = 0.05
DECAY = 0.1
OUTER_RATE = 0.7
OUTER_MOMENTUM = 0.9

MESH = pl.DeviceIdType.MESH
F32 = jnp.float32
BF16 = jnp.bfloat16


def kernel(
    sizes,
    x_hbm, t_hbm, theta_hbm, momentum_hbm, first_hbm, second_hbm,
    result,
    xs, ts, state, weights, part_out, part_in,
    grads, near_a, sum_a, far_a, near_b, sum_b, far_b,
    pool_out, pool_in,
    x_local, x_send, x_recv, t_sems, state_sems,
    part_send, part_recv, send, recv, pool_send, pool_recv,
):
    steps, depths, rows, islands = sizes
    island = lax.axis_index("island")
    replica = lax.axis_index("replica")
    row = lax.axis_index("shard")
    depth, core = replica // 2, replica % 2
    tokens = x_hbm.shape[1]
    width = xs.shape[3]
    head = t_hbm.shape[2]
    half = weights.shape[4]
    key_scale = (depths * 2 * width) ** (-0.5)
    grad_scale = 1.0 / math.sqrt(tokens * 2 * depths * rows)

    def over_rows(offset):
        return {"shard": (row + offset) % rows}

    def over_depths(offset):
        return {"replica": (depth + offset) % depths * 2 + core}

    sibling = {"replica": depth * 2 + 1 - core}

    def over_islands(offset):
        return {"island": (island + offset) % islands}

    def remote(source, target, send_sem, recv_sem, where):
        return pltpu.make_async_remote_copy(
            src_ref=source, dst_ref=target, send_sem=send_sem, recv_sem=recv_sem,
            device_id=where, device_id_type=MESH,
        )

    barrier = pltpu.get_barrier_semaphore()
    greeted = [over_rows(k) for k in range(1, rows)] + [over_depths(k) for k in range(1, depths)]
    greeted += [sibling] + [over_islands(k) for k in range(1, islands)]
    for where in greeted:
        pl.semaphore_signal(barrier, inc=1, device_id=where, device_id_type=MESH)

    def load(k, source):
        return pltpu.make_async_copy(source, state.at[k], state_sems.at[k])

    loads = [load(0, theta_hbm), load(1, momentum_hbm), load(2, first_hbm), load(3, second_hbm)]
    loads[0].start()
    own_tokens = pl.ds(pl.multiple_of(core * tokens, tokens), tokens)

    def x_columns(z, which):
        return pl.ds(pl.multiple_of((z * 2 + which) * width, width), width)

    def x_mine(s, z):
        return pltpu.make_async_copy(
            x_hbm.at[s, :, x_columns(z, core)], xs.at[s, z, own_tokens], x_local.at[s, z]
        )

    def x_theirs(s, z):
        return remote(
            x_hbm.at[s, :, x_columns(z, 1 - core)], xs.at[s, z, own_tokens],
            x_send.at[s, z], x_recv.at[s, z], sibling,
        )

    t_mine = pltpu.make_async_copy(t_hbm, ts.at[:, own_tokens], t_sems.at[0])
    t_theirs = remote(t_hbm, ts.at[:, own_tokens], t_sems.at[1], t_sems.at[2], sibling)
    for z in range(depths):
        x_mine(0, z).start()
    t_mine.start()
    for k in (1, 2, 3):
        loads[k].start()
    for s in range(1, steps):
        for z in range(depths):
            x_mine(s, z).start()

    def gather_rows(s, k):
        block = weights.at[s, depth, row]
        return remote(block, block, send.at[s, 0, k - 1], recv.at[s, 0, k - 1], over_rows(k))

    def gather_depths(s, k):
        block, i = weights.at[s, depth, row], rows + k - 2
        return remote(block, block, send.at[s, 0, i], recv.at[s, 0, i], over_depths(k))

    relay_a, relay_b = rows + depths - 2, rows + depths - 1

    def on_from_rows(s, k):
        gather_rows(s, k).wait_recv()
        block = weights.at[s, depth, (row + rows - k) % rows, 0]
        for m in far_depths:
            remote(block, block, send.at[s, 0, relay_a], recv.at[s, 0, relay_a], over_depths(m)).start()

    def on_from_depths(s, k):
        gather_depths(s, k).wait_recv()
        block = weights.at[s, (depth + depths - k) % depths, row, 1]
        for m in far_rows:
            remote(block, block, send.at[s, 0, relay_b], recv.at[s, 0, relay_b], over_rows(m)).start()

    def relayed(s):
        block = weights.at[s, 0:depths - 1, 0:rows - 1, 0]
        return [
            remote(block, block, send.at[s, 0, i], recv.at[s, 0, i], sibling) for i in (relay_a, relay_b)
        ]

    def scatter_depths(s, j, k):
        return remote(
            grads.at[s, (depth + k) % depths, (row + j) % rows, 0], near_a.at[s, k - 1, j],
            send.at[s, 1, 0], recv.at[s, 1, j], over_depths(k),
        )

    def scatter_rows(s, j, k):
        return remote(
            grads.at[s, (depth + j) % depths, (row + k) % rows, 1], near_b.at[s, k - 1, j],
            send.at[s, 1, 1], recv.at[s, 1, rows + j], over_rows(k),
        )

    def scatter_far_a(s, k):
        i = rows + depths + k - 1
        return remote(sum_a.at[s, k], far_a.at[s, k - 1], send.at[s, 1, i], recv.at[s, 1, i], over_rows(k))

    def scatter_far_b(s, k):
        i = 2 * rows + depths + k - 2
        return remote(sum_b.at[s, k], far_b.at[s, k - 1], send.at[s, 1, i], recv.at[s, 1, i], over_depths(k))

    def combine_a(s, j):
        block = near_a.at[s, :, j]
        remote(block, block, send.at[s, 1, 0], recv.at[s, 1, j], sibling).wait_recv()
        total = grads[s, depth, (row + j) % rows, 0].astype(F32)
        for k in range(depths - 1):
            total += near_a[s, k, j].astype(F32)
        if j == 0:
            return total
        sum_a[s, j] = total.astype(BF16)
        scatter_far_a(s, j).start()

    def combine_b(s, j):
        block = near_b.at[s, :, j]
        remote(block, block, send.at[s, 1, 1], recv.at[s, 1, rows + j], sibling).wait_recv()
        total = grads[s, (depth + j) % depths, row, 1].astype(F32)
        for k in range(rows - 1):
            total += near_b[s, k, j].astype(F32)
        if j == 0:
            return total
        sum_b[s, j] = total.astype(BF16)
        scatter_far_b(s, j).start()

    def far_first(count):
        return sorted(range(1, count), key=lambda k: (-min(k, count - k), k))

    far_rows, far_depths = far_first(rows), far_first(depths)
    near_rows, near_depths = far_rows[::-1], far_depths[::-1]

    def start(copies):
        for copy in copies:
            copy.start()

    def arrive(copies):
        for copy in copies:
            copy.wait_recv()

    loads[0].wait()
    weights[0, depth, row] = state[0].astype(BF16)
    pl.semaphore_wait(barrier, len(greeted))

    for s in range(steps):
        start([gather_depths(s, k) for k in near_depths] + [gather_rows(s, k) for k in near_rows])
        if s == 0:
            for z in range(depths):
                x_theirs(0, z).start()
            t_theirs.start()
        hops = [(min(k, rows - k), 0, k) for k in near_rows] + [(2 * min(k, depths - k), 1, k) for k in near_depths]
        for _, along, k in sorted(hops):
            (on_from_depths if along else on_from_rows)(s, k)
        if s == 0:
            for later in range(1, steps):
                for z in range(depths):
                    x_theirs(later, z).start()
            t_mine.wait()
            t_theirs.wait_recv()
        for z in range(depths):
            x_mine(s, z).wait()
            x_theirs(s, z).wait_recv()
        arrive(relayed(s))

        def part(p):
            block = part_out.at[s, pl.ds(p * tokens, tokens)]
            return remote(
                block, part_in.at[s, pl.ds(p * tokens, tokens)],
                part_send.at[s, p], part_recv.at[s, p], sibling,
            )

        for p in range(2):
            total = jnp.zeros((tokens, head), F32)
            for z in range(depths):
                total += jnp.dot(
                    xs[s, z, p * tokens:(p + 1) * tokens],
                    weights[s, z].reshape(width, head),
                    preferred_element_type=F32,
                )
            part_out[s, p * tokens:(p + 1) * tokens] = total
            part(p).start()
        arrive([part(0), part(1)])
        projected = (part_out[s] + part_in[s]) * key_scale
        residual = (projected - ts[s].astype(F32)).astype(BF16)

        early, late = far_rows[:rows // 2 - 1], far_rows[rows // 2 - 1:] + [0]
        for z in far_depths + [0]:
            at = (depth + z) % depths
            gradient = lax.dot_general(
                xs[s, at], residual, (((0,), (0,)), ((), ())), preferred_element_type=F32
            ) * grad_scale
            grads[s, at] = gradient.astype(BF16).reshape(rows, 2, half, head)
            if z > 0:
                start([scatter_depths(s, j, z) for j in early])
            start([scatter_rows(s, z, k) for k in far_rows])
        start([scatter_depths(s, j, z) for j in late for z in far_depths])
        if s == 0:
            for k in (1, 2, 3):
                loads[k].wait()
        order = [(min(j, rows - j), 0, j) for j in range(rows)] + [(2 * min(j, depths - j), 1, j) for j in range(depths)]
        totals = {}
        for _, along, j in sorted(order, reverse=True):
            totals[along] = (combine_b if along else combine_a)(s, j)

        def update(part_index, gradient):
            parameters = state[0 if s == 0 else 4, part_index]
            first = BETA_ONE * state[2, part_index] + (1.0 - BETA_ONE) * gradient
            second = BETA_TWO * state[3, part_index] + (1.0 - BETA_TWO) * gradient * gradient
            parameters = parameters - INNER_RATE * (
                first / (jnp.sqrt(second) + EPSILON) + DECAY * parameters
            )
            state[2, part_index] = first
            state[3, part_index] = second
            state[4, part_index] = parameters
            if s < steps - 1:
                weights[s + 1, depth, row, part_index] = parameters.astype(BF16)

        for k in near_rows:
            scatter_far_a(s, k).wait_recv()
            totals[0] += far_a[s, k - 1].astype(F32)
        update(0, totals[0])
        for k in near_depths:
            scatter_far_b(s, k).wait_recv()
            totals[1] += far_b[s, k - 1].astype(F32)
        update(1, totals[1])

    moved = state[0] - state[4]
    pool_out[...] = moved.astype(BF16)

    def pool(k):
        return remote(
            pool_out, pool_in.at[k - 1], pool_send.at[k - 1], pool_recv.at[k - 1], over_islands(k)
        )

    pools = [pool(k) for k in range(1, islands)]
    start(pools)

    def store(k, source):
        return pltpu.make_async_copy(source, result.at[k], state_sems.at[k])

    stores = [store(2, state.at[2]), store(3, state.at[3])]
    start(stores)
    for z in range(depths):
        for s in range(steps):
            x_theirs(s, z).wait_send()
    t_theirs.wait_send()
    for s in range(steps):
        for p in range(2):
            block = part_out.at[s, pl.ds(p * tokens, tokens)]
            remote(block, block, part_send.at[s, p], part_recv.at[s, p], sibling).wait_send()
        for k in near_rows:
            gather_rows(s, k).wait_send()
            scatter_far_a(s, k).wait_send()
        for k in near_depths:
            gather_depths(s, k).wait_send()
            scatter_far_b(s, k).wait_send()
        for copy in relayed(s):
            copy.wait_send()
        block = grads.at[s, 0:depths - 1, :, 0]
        remote(block, block, send.at[s, 1, 0], recv.at[s, 1, 0], sibling).wait_send()
        block = grads.at[s, :, 0:rows - 1, 1]
        remote(block, block, send.at[s, 1, 1], recv.at[s, 1, 0], sibling).wait_send()
    arrive(pools)
    total = moved
    for k in range(islands - 1):
        total += pool_in[k].astype(F32)
    pseudo_grad = total / islands
    momentum_new = OUTER_MOMENTUM * state[1] + pseudo_grad
    state[1] = momentum_new
    state[4] = state[0] - OUTER_RATE * (pseudo_grad + OUTER_MOMENTUM * momentum_new)
    last = [store(0, state.at[4]), store(1, state.at[1])]
    start(last)
    for copy in pools:
        copy.wait_send()
    for copy in stores + last:
        copy.wait()


def part_results(result, theta_out, momentum_out, first_out, second_out, sems):
    outs = (theta_out, momentum_out, first_out, second_out)
    copies = [pltpu.make_async_copy(result.at[k], out, sems.at[k]) for k, out in enumerate(outs)]
    for copy in copies:
        copy.start()
    for copy in copies:
        copy.wait()


def per_device(inputs, targets, theta, momentum, first_moment, second_moment):
    steps, tokens, _ = inputs.shape
    block, head = theta.shape
    islands = lax.axis_size("island")
    depths, rows = lax.axis_size("replica") // 2, lax.axis_size("shard")
    half, width = block // 2, rows * block
    split = (2, half, head)
    copies = 2 * (rows + depths) + rows
    dma = pltpu.SemaphoreType.DMA
    in_hbm = pl.BlockSpec(memory_space=pltpu.HBM)
    vmem = pltpu.VMEM
    result = pl.pallas_call(
        functools.partial(kernel, (steps, depths, rows, islands)),
        out_shape=jax.ShapeDtypeStruct((4,) + split, F32),
        in_specs=[in_hbm] * 6,
        out_specs=in_hbm,
        scratch_shapes=[
            vmem((steps, depths, 2 * tokens, width), BF16),
            vmem((steps, 2 * tokens, head), BF16),
            vmem((5,) + split, F32),
            vmem((steps, depths, rows) + split, BF16),
            vmem((steps, 2 * tokens, head), F32),
            vmem((steps, 2 * tokens, head), F32),
            vmem((steps, depths, rows) + split, BF16),
            vmem((steps, depths - 1, rows, half, head), BF16),
            vmem((steps, rows, half, head), BF16),
            vmem((steps, rows - 1, half, head), BF16),
            vmem((steps, rows - 1, depths, half, head), BF16),
            vmem((steps, depths, half, head), BF16),
            vmem((steps, depths - 1, half, head), BF16),
            vmem(split, BF16),
            vmem((islands - 1,) + split, BF16),
            dma((steps, depths)), dma((steps, depths)), dma((steps, depths)),
            dma((3,)), dma((4,)),
            dma((steps, 2)), dma((steps, 2)),
            dma((steps, 2, copies)), dma((steps, 2, copies)),
            dma((islands - 1,)), dma((islands - 1,)),
        ],
        compiler_params=pltpu.CompilerParams(
            collective_id=0, has_side_effects=True, vmem_limit_bytes=60 * 1024 * 1024
        ),
    )(
        inputs, targets, theta.reshape(split), momentum.reshape(split),
        first_moment.reshape(split), second_moment.reshape(split),
    )
    outs = pl.pallas_call(
        part_results,
        out_shape=[jax.ShapeDtypeStruct(split, F32)] * 4,
        in_specs=[in_hbm],
        out_specs=[in_hbm] * 4,
        scratch_shapes=[dma((4,))],
    )(result)
    theta_new, momentum_new, first, second = [out.reshape(block, head) for out in outs]
    return (theta_new, momentum_new, first[None], second[None])


def solution(mesh):
    in_specs = (
        P(None, ("island", "replica", "shard"), None),
        P(None, ("island", "replica", "shard"), None),
        P(("replica", "shard"), None),
        P(("replica", "shard"), None),
        P("island", ("replica", "shard"), None),
        P("island", ("replica", "shard"), None),
    )
    out_specs = (
        P(("replica", "shard"), None),
        P(("replica", "shard"), None),
        P("island", ("replica", "shard"), None),
        P("island", ("replica", "shard"), None),
    )
    return jax.shard_map(
        per_device, mesh=mesh, in_specs=in_specs, out_specs=out_specs, check_vma=False
    )
```

```python
import functools
import math

import jax
import jax.numpy as jnp
from jax import lax
from jax.experimental import pallas as pl
from jax.experimental.pallas import tpu as pltpu
from jax.sharding import PartitionSpec as P

BETA_ONE = 0.9
BETA_TWO = 0.95
EPSILON = 1e-08
INNER_RATE = 0.05
DECAY = 0.1
OUTER_RATE = 0.7
OUTER_MOMENTUM = 0.9

MESH = pl.DeviceIdType.MESH
F32 = jnp.float32
BF16 = jnp.bfloat16


def kernel(
    sizes,
    x_hbm, t_hbm, theta_hbm, momentum_hbm, first_hbm, second_hbm,
    result,
    xs, ts, state, weights, part_out, part_in,
    grads, near_a, sum_a, far_a, near_b, sum_b, far_b,
    pool_out, pool_in,
    x_local, x_send, x_recv, t_sems, state_sems,
    part_send, part_recv, send, recv, pool_send, pool_recv,
):
    steps, depths, rows, islands = sizes
    island = lax.axis_index("island")
    replica = lax.axis_index("replica")
    row = lax.axis_index("shard")
    depth, core = replica // 2, replica % 2
    tokens = x_hbm.shape[1]
    width = xs.shape[3]
    head = t_hbm.shape[2]
    half = weights.shape[4]
    key_scale = (depths * 2 * width) ** (-0.5)
    grad_scale = 1.0 / math.sqrt(tokens * 2 * depths * rows)

    def over_rows(offset):
        return {"shard": (row + offset) % rows}

    def over_depths(offset):
        return {"replica": (depth + offset) % depths * 2 + core}

    sibling = {"replica": depth * 2 + 1 - core}

    def over_islands(offset):
        return {"island": (island + offset) % islands}

    def remote(source, target, send_sem, recv_sem, where):
        return pltpu.make_async_remote_copy(
            src_ref=source, dst_ref=target, send_sem=send_sem, recv_sem=recv_sem,
            device_id=where, device_id_type=MESH,
        )

    barrier = pltpu.get_barrier_semaphore()
    greeted = [over_rows(k) for k in range(1, rows)] + [over_depths(k) for k in range(1, depths)]
    greeted += [sibling] + [over_islands(k) for k in range(1, islands)]
    for where in greeted:
        pl.semaphore_signal(barrier, inc=1, device_id=where, device_id_type=MESH)

    def load(k, source):
        return pltpu.make_async_copy(source, state.at[k], state_sems.at[k])

    loads = [load(0, theta_hbm), load(1, momentum_hbm), load(2, first_hbm), load(3, second_hbm)]
    loads[0].start()
    own_tokens = pl.ds(pl.multiple_of(core * tokens, tokens), tokens)

    def x_columns(z, which):
        return pl.ds(pl.multiple_of((z * 2 + which) * width, width), width)

    def x_mine(s, z):
        return pltpu.make_async_copy(
            x_hbm.at[s, :, x_columns(z, core)], xs.at[s, z, own_tokens], x_local.at[s, z]
        )

    def x_theirs(s, z):
        return remote(
            x_hbm.at[s, :, x_columns(z, 1 - core)], xs.at[s, z, own_tokens],
            x_send.at[s, z], x_recv.at[s, z], sibling,
        )

    t_mine = pltpu.make_async_copy(t_hbm, ts.at[:, own_tokens], t_sems.at[0])
    t_theirs = remote(t_hbm, ts.at[:, own_tokens], t_sems.at[1], t_sems.at[2], sibling)
    for z in range(depths):
        x_mine(0, z).start()
    t_mine.start()
    for k in (1, 2, 3):
        loads[k].start()
    for s in range(1, steps):
        for z in range(depths):
            x_mine(s, z).start()

    def gather_rows(s, k):
        block = weights.at[s, depth, row]
        return remote(block, block, send.at[s, 0, k - 1], recv.at[s, 0, k - 1], over_rows(k))

    def gather_depths(s, k):
        block, i = weights.at[s, depth, row], rows + k - 2
        return remote(block, block, send.at[s, 0, i], recv.at[s, 0, i], over_depths(k))

    relay_a, relay_b = rows + depths - 2, rows + depths - 1

    def on_from_rows(s, k):
        gather_rows(s, k).wait_recv()
        block = weights.at[s, depth, (row + rows - k) % rows, 0]
        for m in far_depths:
            remote(block, block, send.at[s, 0, relay_a], recv.at[s, 0, relay_a], over_depths(m)).start()

    def on_from_depths(s, k):
        gather_depths(s, k).wait_recv()
        block = weights.at[s, (depth + depths - k) % depths, row, 1]
        for m in far_rows:
            remote(block, block, send.at[s, 0, relay_b], recv.at[s, 0, relay_b], over_rows(m)).start()

    def relayed(s):
        block = weights.at[s, 0:depths - 1, 0:rows - 1, 0]
        return [
            remote(block, block, send.at[s, 0, i], recv.at[s, 0, i], sibling) for i in (relay_a, relay_b)
        ]

    def scatter_depths(s, j, k):
        return remote(
            grads.at[s, (depth + k) % depths, (row + j) % rows, 0], near_a.at[s, k - 1, j],
            send.at[s, 1, 0], recv.at[s, 1, j], over_depths(k),
        )

    def scatter_rows(s, j, k):
        return remote(
            grads.at[s, (depth + j) % depths, (row + k) % rows, 1], near_b.at[s, k - 1, j],
            send.at[s, 1, 1], recv.at[s, 1, rows + j], over_rows(k),
        )

    def scatter_far_a(s, k):
        i = rows + depths + k - 1
        return remote(sum_a.at[s, k], far_a.at[s, k - 1], send.at[s, 1, i], recv.at[s, 1, i], over_rows(k))

    def scatter_far_b(s, k):
        i = 2 * rows + depths + k - 2
        return remote(sum_b.at[s, k], far_b.at[s, k - 1], send.at[s, 1, i], recv.at[s, 1, i], over_depths(k))

    def combine_a(s, j):
        block = near_a.at[s, :, j]
        remote(block, block, send.at[s, 1, 0], recv.at[s, 1, j], sibling).wait_recv()
        total = grads[s, depth, (row + j) % rows, 0].astype(F32)
        for k in range(depths - 1):
            total += near_a[s, k, j].astype(F32)
        if j == 0:
            return total
        sum_a[s, j] = total.astype(BF16)
        scatter_far_a(s, j).start()

    def combine_b(s, j):
        block = near_b.at[s, :, j]
        remote(block, block, send.at[s, 1, 1], recv.at[s, 1, rows + j], sibling).wait_recv()
        total = grads[s, (depth + j) % depths, row, 1].astype(F32)
        for k in range(rows - 1):
            total += near_b[s, k, j].astype(F32)
        if j == 0:
            return total
        sum_b[s, j] = total.astype(BF16)
        scatter_far_b(s, j).start()

    def far_first(count):
        return sorted(range(1, count), key=lambda k: (-min(k, count - k), k))

    far_rows, far_depths = far_first(rows), far_first(depths)
    near_rows, near_depths = far_rows[::-1], far_depths[::-1]

    def start(copies):
        for copy in copies:
            copy.start()

    def arrive(copies):
        for copy in copies:
            copy.wait_recv()

    loads[0].wait()
    weights[0, depth, row] = state[0].astype(BF16)
    pl.semaphore_wait(barrier, len(greeted))

    for s in range(steps):
        start([gather_depths(s, k) for k in near_depths] + [gather_rows(s, k) for k in near_rows])
        if s == 0:
            for z in range(depths):
                x_theirs(0, z).start()
            t_theirs.start()
        hops = [(min(k, rows - k), 0, k) for k in near_rows] + [(2 * min(k, depths - k), 1, k) for k in near_depths]
        for _, along, k in sorted(hops):
            (on_from_depths if along else on_from_rows)(s, k)
        if s == 0:
            for later in range(1, steps):
                for z in range(depths):
                    x_theirs(later, z).start()
            t_mine.wait()
            t_theirs.wait_recv()
        for z in range(depths):
            x_mine(s, z).wait()
            x_theirs(s, z).wait_recv()
        arrive(relayed(s))

        def part(p):
            block = part_out.at[s, pl.ds(p * tokens, tokens)]
            return remote(
                block, part_in.at[s, pl.ds(p * tokens, tokens)],
                part_send.at[s, p], part_recv.at[s, p], sibling,
            )

        for p in range(2):
            total = jnp.zeros((tokens, head), F32)
            for z in range(depths):
                total += jnp.dot(
                    xs[s, z, p * tokens:(p + 1) * tokens],
                    weights[s, z].reshape(width, head),
                    preferred_element_type=F32,
                )
            part_out[s, p * tokens:(p + 1) * tokens] = total
            part(p).start()
        arrive([part(0), part(1)])
        projected = (part_out[s] + part_in[s]) * key_scale
        residual = (projected - ts[s].astype(F32)).astype(BF16)

        early, late = far_rows[:rows // 2 - 1], far_rows[rows // 2 - 1:] + [0]
        for z in far_depths + [0]:
            at = (depth + z) % depths
            gradient = lax.dot_general(
                xs[s, at], residual, (((0,), (0,)), ((), ())), preferred_element_type=F32
            ) * grad_scale
            grads[s, at] = gradient.astype(BF16).reshape(rows, 2, half, head)
            if z > 0:
                start([scatter_depths(s, j, z) for j in early])
            start([scatter_rows(s, z, k) for k in far_rows])
        start([scatter_depths(s, j, z) for j in late for z in far_depths])
        if s == 0:
            for k in (1, 2, 3):
                loads[k].wait()
        order = [(min(j, rows - j), 0, j) for j in range(rows)] + [(2 * min(j, depths - j), 1, j) for j in range(depths)]
        totals = {}
        for _, along, j in sorted(order, reverse=True):
            totals[along] = (combine_b if along else combine_a)(s, j)

        def update(part_index, gradient):
            parameters = state[0 if s == 0 else 4, part_index]
            first = BETA_ONE * state[2, part_index] + (1.0 - BETA_ONE) * gradient
            second = BETA_TWO * state[3, part_index] + (1.0 - BETA_TWO) * gradient * gradient
            parameters = parameters - INNER_RATE * (
                first / (jnp.sqrt(second) + EPSILON) + DECAY * parameters
            )
            state[2, part_index] = first
            state[3, part_index] = second
            state[4, part_index] = parameters
            if s < steps - 1:
                weights[s + 1, depth, row, part_index] = parameters.astype(BF16)

        for k in near_rows:
            scatter_far_a(s, k).wait_recv()
            totals[0] += far_a[s, k - 1].astype(F32)
        update(0, totals[0])
        for k in near_depths:
            scatter_far_b(s, k).wait_recv()
            totals[1] += far_b[s, k - 1].astype(F32)
        update(1, totals[1])

    moved = state[0] - state[4]
    pool_out[...] = moved.astype(BF16)

    def pool(k):
        return remote(
            pool_out, pool_in.at[k - 1], pool_send.at[k - 1], pool_recv.at[k - 1], over_islands(k)
        )

    pools = [pool(k) for k in range(1, islands)]
    start(pools)

    result[2] = state[2]
    result[3] = state[3]
    for z in range(depths):
        for s in range(steps):
            x_theirs(s, z).wait_send()
    t_theirs.wait_send()
    for s in range(steps):
        for p in range(2):
            block = part_out.at[s, pl.ds(p * tokens, tokens)]
            remote(block, block, part_send.at[s, p], part_recv.at[s, p], sibling).wait_send()
        for k in near_rows:
            gather_rows(s, k).wait_send()
            scatter_far_a(s, k).wait_send()
        for k in near_depths:
            gather_depths(s, k).wait_send()
            scatter_far_b(s, k).wait_send()
        for copy in relayed(s):
            copy.wait_send()
        block = grads.at[s, 0:depths - 1, :, 0]
        remote(block, block, send.at[s, 1, 0], recv.at[s, 1, 0], sibling).wait_send()
        block = grads.at[s, :, 0:rows - 1, 1]
        remote(block, block, send.at[s, 1, 1], recv.at[s, 1, 0], sibling).wait_send()
    arrive(pools)
    total = moved
    for k in range(islands - 1):
        total += pool_in[k].astype(F32)
    pseudo_grad = total / islands
    momentum_new = OUTER_MOMENTUM * state[1] + pseudo_grad
    result[1] = momentum_new
    result[0] = state[0] - OUTER_RATE * (pseudo_grad + OUTER_MOMENTUM * momentum_new)
    for copy in pools:
        copy.wait_send()


def part_results(result, theta_out, momentum_out, first_out, second_out, sems):
    outs = (theta_out, momentum_out, first_out, second_out)
    copies = [pltpu.make_async_copy(result.at[k], out, sems.at[k]) for k, out in enumerate(outs)]
    for copy in copies:
        copy.start()
    for copy in copies:
        copy.wait()


def per_device(inputs, targets, theta, momentum, first_moment, second_moment):
    steps, tokens, _ = inputs.shape
    block, head = theta.shape
    islands = lax.axis_size("island")
    depths, rows = lax.axis_size("replica") // 2, lax.axis_size("shard")
    half, width = block // 2, rows * block
    split = (2, half, head)
    copies = 2 * (rows + depths) + rows
    dma = pltpu.SemaphoreType.DMA
    in_hbm = pl.BlockSpec(memory_space=pltpu.HBM)
    in_vmem = pl.BlockSpec(memory_space=pltpu.VMEM)
    vmem = pltpu.VMEM
    result = pl.pallas_call(
        functools.partial(kernel, (steps, depths, rows, islands)),
        out_shape=pltpu.VMEM((4,) + split, F32),
        in_specs=[in_hbm] * 6,
        out_specs=in_vmem,
        scratch_shapes=[
            vmem((steps, depths, 2 * tokens, width), BF16),
            vmem((steps, 2 * tokens, head), BF16),
            vmem((5,) + split, F32),
            vmem((steps, depths, rows) + split, BF16),
            vmem((steps, 2 * tokens, head), F32),
            vmem((steps, 2 * tokens, head), F32),
            vmem((steps, depths, rows) + split, BF16),
            vmem((steps, depths - 1, rows, half, head), BF16),
            vmem((steps, rows, half, head), BF16),
            vmem((steps, rows - 1, half, head), BF16),
            vmem((steps, rows - 1, depths, half, head), BF16),
            vmem((steps, depths, half, head), BF16),
            vmem((steps, depths - 1, half, head), BF16),
            vmem(split, BF16),
            vmem((islands - 1,) + split, BF16),
            dma((steps, depths)), dma((steps, depths)), dma((steps, depths)),
            dma((3,)), dma((4,)),
            dma((steps, 2)), dma((steps, 2)),
            dma((steps, 2, copies)), dma((steps, 2, copies)),
            dma((islands - 1,)), dma((islands - 1,)),
        ],
        compiler_params=pltpu.CompilerParams(
            collective_id=0, has_side_effects=True, vmem_limit_bytes=60 * 1024 * 1024
        ),
    )(
        inputs, targets, theta.reshape(split), momentum.reshape(split),
        first_moment.reshape(split), second_moment.reshape(split),
    )
    outs = pl.pallas_call(
        part_results,
        out_shape=[jax.ShapeDtypeStruct(split, F32)] * 4,
        in_specs=[in_vmem],
        out_specs=[in_hbm] * 4,
        scratch_shapes=[dma((4,))],
        compiler_params=pltpu.CompilerParams(vmem_limit_bytes=1024 * 1024),
    )(result)
    theta_new, momentum_new, first, second = [out.reshape(block, head) for out in outs]
    return (theta_new, momentum_new, first[None], second[None])


def solution(mesh):
    in_specs = (
        P(None, ("island", "replica", "shard"), None),
        P(None, ("island", "replica", "shard"), None),
        P(("replica", "shard"), None),
        P(("replica", "shard"), None),
        P("island", ("replica", "shard"), None),
        P("island", ("replica", "shard"), None),
    )
    out_specs = (
        P(("replica", "shard"), None),
        P(("replica", "shard"), None),
        P("island", ("replica", "shard"), None),
        P("island", ("replica", "shard"), None),
    )
    return jax.shard_map(
        per_device, mesh=mesh, in_specs=in_specs, out_specs=out_specs, check_vma=False
    )
```

```python
import functools
import math

import jax
import jax.numpy as jnp
from jax import lax
from jax.experimental import pallas as pl
from jax.experimental.pallas import tpu as pltpu
from jax.sharding import PartitionSpec as P

BETA_ONE = 0.9
BETA_TWO = 0.95
EPSILON = 1e-08
INNER_RATE = 0.05
DECAY = 0.1
OUTER_RATE = 0.7
OUTER_MOMENTUM = 0.9

MESH = pl.DeviceIdType.MESH
F32 = jnp.float32
BF16 = jnp.bfloat16


def far_first(count):
    return sorted(range(1, count), key=lambda k: (-min(k, count - k), k))


def kernel(
    sizes,
    x_hbm, t_hbm, theta_hbm, momentum_hbm, first_hbm, second_hbm,
    result,
    xs, ts, state, weights, part_out, part_in,
    grads, near_a, sum_a, far_a, near_b, sum_b, far_b,
    pool_out, pool_in,
    x_local, x_send, x_recv, t_sems, state_sems,
    part_send, part_recv, send, recv, pool_sems,
):
    steps, depths, rows, islands = sizes
    island = lax.axis_index("island")
    replica = lax.axis_index("replica")
    row = lax.axis_index("shard")
    depth, core = replica // 2, replica % 2
    tokens = x_hbm.shape[1]
    width = xs.shape[3]
    head = t_hbm.shape[2]
    half = weights.shape[3]
    key_scale = (depths * 2 * width) ** (-0.5)
    grad_scale = 1.0 / math.sqrt(tokens * 2 * depths * rows)

    def over_rows(offset):
        return {"shard": (row + offset) % rows}

    def over_depths(offset):
        return {"replica": (depth + offset) % depths * 2 + core}

    sibling = {"replica": depth * 2 + 1 - core}

    def over_islands(offset):
        return {"island": (island + offset) % islands}

    def remote(source, target, send_sem, recv_sem, where):
        return pltpu.make_async_remote_copy(
            src_ref=source, dst_ref=target, send_sem=send_sem, recv_sem=recv_sem,
            device_id=where, device_id_type=MESH,
        )

    barrier = pltpu.get_barrier_semaphore()
    far_rows, far_depths = far_first(rows), far_first(depths)
    near_rows, near_depths = far_rows[::-1], far_depths[::-1]
    outer, inner = far_rows[:3], far_rows[3:]
    greeted = [over_rows(k) for k in far_rows] + [over_depths(k) for k in far_depths]
    greeted += [sibling] + [over_islands(k) for k in range(1, islands)]
    for where in greeted:
        pl.semaphore_signal(barrier, inc=1, device_id=where, device_id_type=MESH)

    def load(k, source):
        return pltpu.make_async_copy(source, state.at[k], state_sems.at[min(k, 1)])

    def loaded(block, sem):
        pltpu.make_async_copy(block, block, sem).wait()

    loads = [load(0, theta_hbm), load(1, momentum_hbm), load(2, first_hbm), load(3, second_hbm)]
    loads[0].start()
    own_tokens = pl.ds(pl.multiple_of(core * tokens, tokens), tokens)

    def x_columns(z, which):
        return pl.ds(pl.multiple_of((z * 2 + which) * width, width), width)

    def x_mine(s, z):
        return pltpu.make_async_copy(
            x_hbm.at[s, :, x_columns(z, core)], xs.at[s, z, own_tokens], x_local.at[s]
        )

    def x_theirs(s, z):
        return remote(
            x_hbm.at[s, :, x_columns(z, 1 - core)], xs.at[s, z, own_tokens],
            x_send.at[0], x_recv.at[s], sibling,
        )

    t_mine = pltpu.make_async_copy(t_hbm, ts.at[:, own_tokens], t_sems.at[0])
    t_theirs = remote(t_hbm, ts.at[:, own_tokens], t_sems.at[1], t_sems.at[2], sibling)
    for z in range(depths):
        x_mine(0, z).start()
    t_mine.start()
    for k in (1, 2, 3):
        loads[k].start()
    for s in range(1, steps):
        for z in range(depths):
            x_mine(s, z).start()

    at_rows, at_depths = 0, rows // 2
    at_a = at_depths + depths // 2
    at_b = at_a + depths - 1
    at_near_a = at_b + depths
    at_near_b = at_near_a + rows
    at_far = at_near_b + depths

    def near_send(s, part, i, where):
        block = weights.at[s, depth * rows + row, part]
        return remote(block, block, send.at[s, 0], recv.at[s, i], where)

    def gather_rows(s, k):
        return near_send(s, 0, at_rows + min(k, rows - k) - 1, over_rows(k))

    def gather_depths(s, k):
        return near_send(s, 1, at_depths + min(k, depths - k) - 1, over_depths(k))

    def received(block, sem):
        remote(block, block, send.at[0, 0], sem, sibling).wait_recv()

    def near_received(s, first, distance, count):
        copies = len({distance, count - distance})
        received(weights.at[s, 0:copies, 0], recv.at[s, first + distance - 1])

    def on_from_row(s, k, targets):
        block = weights.at[s, depth * rows + (row + rows - k) % rows, 0]
        for m in targets:
            remote(block, block, send.at[s, 0], recv.at[s, at_a + m - 1], over_depths(m)).start()

    def on_from_depth(s, k, targets):
        block = weights.at[s, (depth + depths - k) % depths * rows + row, 1]
        for m in targets:
            remote(block, block, send.at[s, 0], recv.at[s, at_b + k], over_rows(m)).start()

    def depth_received(s, k):
        if k > 0:
            received(weights.at[s, 0:rows, 0], recv.at[s, at_a + k - 1])
        received(weights.at[s, 0:rows - 1, 1], recv.at[s, at_b + k])

    def scatter_depths(s, j, k):
        return remote(
            grads.at[s, (depth + k) % depths, (row + j) % rows, 0], near_a.at[s, k - 1, j],
            send.at[s, 1], recv.at[s, at_near_a + j], over_depths(k),
        )

    def scatter_rows(s, j, k):
        return remote(
            grads.at[s, (depth + j) % depths, (row + k) % rows, 1], near_b.at[s, k - 1, j],
            send.at[s, 1], recv.at[s, at_near_b + j], over_rows(k),
        )

    def scatter_far_a(s, k):
        return remote(sum_a.at[s, k], far_a.at[s, k - 1], send.at[s, 1], recv.at[s, at_far], over_rows(k))

    def scatter_far_b(s, k):
        return remote(sum_b.at[s, k], far_b.at[s, k - 1], send.at[s, 1], recv.at[s, at_far + 1], over_depths(k))

    def combine_a(s, j):
        received(near_a.at[s, :, j], recv.at[s, at_near_a + j])
        total = grads[s, depth, (row + j) % rows, 0].astype(F32)
        for k in range(depths - 1):
            total += near_a[s, k, j].astype(F32)
        if j == 0:
            return total
        sum_a[s, j] = total.astype(BF16)
        scatter_far_a(s, j).start()

    def combine_b(s, j):
        received(near_b.at[s, :, j], recv.at[s, at_near_b + j])
        total = grads[s, (depth + j) % depths, row, 1].astype(F32)
        for k in range(rows - 1):
            total += near_b[s, k, j].astype(F32)
        if j == 0:
            return total
        sum_b[s, j] = total.astype(BF16)
        scatter_far_b(s, j).start()

    def gather_start(s, part):
        if part == 0:
            start([gather_rows(s, k) for k in near_rows[:2] + near_rows[6:] + near_rows[2:6]])
        else:
            start([gather_depths(s, k) for k in near_depths])

    def start(copies):
        for copy in copies:
            copy.start()

    def arrive(copies):
        for copy in copies:
            copy.wait_recv()

    near_depth, far_depth = depths > 2, depths // 2
    waits = [(0, 1)] + [(1, 1)] * near_depth + [(0, d) for d in (2, rows // 2, 3) if d < rows // 2 or d == rows // 2 > 1]
    waits = list(dict.fromkeys(waits)) + [(1, far_depth)]

    loads[0].wait()
    weights[0, depth * rows + row] = state[0].astype(BF16)
    pl.semaphore_wait(barrier, len(greeted))
    gather_start(0, 0)
    gather_start(0, 1)

    for s in range(steps):
        on_from_row(s, 0, far_depths)
        on_from_depth(s, 0, far_rows)
        if s == 0:
            for z in range(depths):
                x_theirs(0, z).start()
            t_theirs.start()
        for along, d in waits:
            near_received(s, at_depths if along else at_rows, d, depths if along else rows)
            for k in sorted({d, (depths if along else rows) - d}):
                if along:
                    on_from_depth(s, k, outer)
                else:
                    on_from_row(s, k, far_depths)
        for k in near_depths:
            on_from_depth(s, k, inner)
        if s == 0:
            for later in range(1, steps):
                for z in range(depths):
                    x_theirs(later, z).start()
            t_mine.wait()
            t_theirs.wait_recv()
        loaded(xs.at[s, :, own_tokens], x_local.at[s])
        received(xs.at[s, :, own_tokens], x_recv.at[s])

        def part(p):
            block = part_out.at[s, pl.ds(p * tokens, tokens)]
            return remote(
                block, part_in.at[s, pl.ds(p * tokens, tokens)], part_send.at[0], part_recv.at[s, p], sibling
            )

        for n, k in enumerate([0] + near_depths):
            z = (depth + depths - k) % depths
            depth_received(s, k)
            block = weights[s, pl.ds(z * rows, rows)].reshape(width, head)
            for p in range(2):
                total = jnp.dot(xs[s, z, p * tokens:(p + 1) * tokens], block, preferred_element_type=F32)
                if n > 0:
                    total += part_out[s, p * tokens:(p + 1) * tokens]
                part_out[s, p * tokens:(p + 1) * tokens] = total
                if n == depths - 1:
                    part(p).start()
        arrive([part(0), part(1)])
        projected = (part_out[s] + part_in[s]) * key_scale
        residual = (projected - ts[s].astype(F32)).astype(BF16)

        if s == 0:
            loaded(state.at[1:4], state_sems.at[1])
        for z in far_depths + [0]:
            at = (depth + z) % depths
            gradient = lax.dot_general(
                xs[s, at], residual, (((0,), (0,)), ((), ())), preferred_element_type=F32
            ) * grad_scale
            grads[s, at] = gradient.astype(BF16).reshape(rows, 2, half, head)
            if z > 0:
                start([scatter_depths(s, j, z) for j in outer])
            if z > 0:
                start([scatter_rows(s, z, k) for k in far_rows])
        start([scatter_depths(s, j, z) for j in inner for z in far_depths])
        combine_a(s, far_rows[0])
        start([scatter_rows(s, 0, k) for k in far_rows])
        combine_b(s, far_depths[0])
        start([scatter_depths(s, 0, z) for z in far_depths])
        rest = [(0, j) for j in far_rows[1:3]] + [(1, j) for j in far_depths[1:2]] + [(0, j) for j in far_rows[3:5]]
        rest += [(1, j) for j in far_depths[2:]] + [(0, j) for j in far_rows[5:]]
        for along, j in rest:
            (combine_b if along else combine_a)(s, j)
        totals = {1: combine_b(s, 0), 0: combine_a(s, 0)}

        def update(part_index, gradient):
            parameters = state[0 if s == 0 else 4, part_index]
            first = BETA_ONE * state[2, part_index] + (1.0 - BETA_ONE) * gradient
            second = BETA_TWO * state[3, part_index] + (1.0 - BETA_TWO) * gradient * gradient
            parameters = parameters - INNER_RATE * (
                first / (jnp.sqrt(second) + EPSILON) + DECAY * parameters
            )
            state[2, part_index] = first
            state[3, part_index] = second
            state[4, part_index] = parameters
            if s < steps - 1:
                weights[s + 1, depth * rows + row, part_index] = parameters.astype(BF16)
                gather_start(s + 1, part_index)

        received(far_a.at[s], recv.at[s, at_far])
        for k in range(rows - 1):
            totals[0] += far_a[s, k].astype(F32)
        update(0, totals[0])
        received(far_b.at[s], recv.at[s, at_far + 1])
        for k in range(depths - 1):
            totals[1] += far_b[s, k].astype(F32)
        update(1, totals[1])

    moved = state[0] - state[4]
    pool_out[...] = moved.astype(BF16)

    def pool(k):
        return remote(
            pool_out, pool_in.at[k - 1], pool_sems.at[0], pool_sems.at[1], over_islands(k)
        )

    pools = [pool(k) for k in range(1, islands)]
    start(pools)

    result[2] = state[2]
    result[3] = state[3]
    def left(block, sem):
        remote(block, block, sem, x_recv.at[0], sibling).wait_send()

    left(xs.at[:, :, own_tokens], x_send.at[0])
    left(ts.at[:, own_tokens], t_sems.at[1])
    left(part_out, part_send.at[0])
    for s in range(steps):
        for sem in (send.at[s, 0], send.at[s, 1]):
            left(weights.at[s, 0:depths * rows - 1], sem)
    received(pool_in, pool_sems.at[1])
    total = moved
    for k in range(islands - 1):
        total += pool_in[k].astype(F32)
    pseudo_grad = total / islands
    momentum_new = OUTER_MOMENTUM * state[1] + pseudo_grad
    result[1] = momentum_new
    result[0] = state[0] - OUTER_RATE * (pseudo_grad + OUTER_MOMENTUM * momentum_new)
    left(pool_in, pool_sems.at[0])


def part_results(result, theta_out, momentum_out, first_out, second_out, sems):
    outs = (theta_out, momentum_out, first_out, second_out)
    copies = [pltpu.make_async_copy(result.at[k], out, sems.at[k]) for k, out in enumerate(outs)]
    for copy in copies:
        copy.start()
    for copy in copies:
        copy.wait()


def per_device(inputs, targets, theta, momentum, first_moment, second_moment):
    steps, tokens, _ = inputs.shape
    block, head = theta.shape
    islands = lax.axis_size("island")
    depths, rows = lax.axis_size("replica") // 2, lax.axis_size("shard")
    half, width = block // 2, rows * block
    split = (2, half, head)
    arrivals = rows // 2 + depths // 2 + depths - 1 + depths + rows + depths + 2
    dma = pltpu.SemaphoreType.DMA
    in_hbm = pl.BlockSpec(memory_space=pltpu.HBM)
    in_vmem = pl.BlockSpec(memory_space=pltpu.VMEM)
    vmem = pltpu.VMEM
    result = pl.pallas_call(
        functools.partial(kernel, (steps, depths, rows, islands)),
        out_shape=pltpu.VMEM((4,) + split, F32),
        in_specs=[in_hbm] * 6,
        out_specs=in_vmem,
        scratch_shapes=[
            vmem((steps, depths, 2 * tokens, width), BF16),
            vmem((steps, 2 * tokens, head), BF16),
            vmem((5,) + split, F32),
            vmem((steps, depths * rows) + split, BF16),
            vmem((steps, 2 * tokens, head), F32),
            vmem((steps, 2 * tokens, head), F32),
            vmem((steps, depths, rows) + split, BF16),
            vmem((steps, depths - 1, rows, half, head), BF16),
            vmem((steps, rows, half, head), BF16),
            vmem((steps, rows - 1, half, head), BF16),
            vmem((steps, rows - 1, depths, half, head), BF16),
            vmem((steps, depths, half, head), BF16),
            vmem((steps, depths - 1, half, head), BF16),
            vmem(split, BF16),
            vmem((islands - 1,) + split, BF16),
            dma((steps,)), dma((1,)), dma((steps,)),
            dma((3,)), dma((2,)),
            dma((1,)), dma((steps, 2)),
            dma((steps, 2)), dma((steps, arrivals)),
            dma((2,)),
        ],
        compiler_params=pltpu.CompilerParams(
            collective_id=0, has_side_effects=True, vmem_limit_bytes=60 * 1024 * 1024
        ),
    )(
        inputs, targets, theta.reshape(split), momentum.reshape(split),
        first_moment.reshape(split), second_moment.reshape(split),
    )
    outs = pl.pallas_call(
        part_results,
        out_shape=[jax.ShapeDtypeStruct(split, F32)] * 4,
        in_specs=[in_vmem],
        out_specs=[in_hbm] * 4,
        scratch_shapes=[dma((4,))],
        compiler_params=pltpu.CompilerParams(vmem_limit_bytes=1024 * 1024),
    )(result)
    theta_new, momentum_new, first, second = [out.reshape(block, head) for out in outs]
    return (theta_new, momentum_new, first[None], second[None])


def solution(mesh):
    in_specs = (
        P(None, ("island", "replica", "shard"), None),
        P(None, ("island", "replica", "shard"), None),
        P(("replica", "shard"), None),
        P(("replica", "shard"), None),
        P("island", ("replica", "shard"), None),
        P("island", ("replica", "shard"), None),
    )
    out_specs = (
        P(("replica", "shard"), None),
        P(("replica", "shard"), None),
        P("island", ("replica", "shard"), None),
        P("island", ("replica", "shard"), None),
    )
    return jax.shard_map(
        per_device, mesh=mesh, in_specs=in_specs, out_specs=out_specs, check_vma=False
    )
```

```python
import functools
import math

import jax
import jax.numpy as jnp
from jax import lax
from jax.experimental import pallas as pl
from jax.experimental.pallas import tpu as pltpu
from jax.sharding import PartitionSpec as P

BETA_ONE = 0.9
BETA_TWO = 0.95
EPSILON = 1e-08
INNER_RATE = 0.05
DECAY = 0.1
OUTER_RATE = 0.7
OUTER_MOMENTUM = 0.9

MESH = pl.DeviceIdType.MESH
F32 = jnp.float32
BF16 = jnp.bfloat16


def far_first(count):
    return sorted(range(1, count), key=lambda k: (-min(k, count - k), k))


def kernel(
    sizes,
    x_hbm, t_hbm, theta_hbm, momentum_hbm, first_hbm, second_hbm,
    result,
    xs, ts, state, weights, part_out, part_in,
    grads, near_a, sum_a, far_a, near_b, sum_b, far_b,
    pool_out, pool_in,
    x_local, x_send, x_recv, t_sems, state_sems,
    part_send, part_recv, send, recv, pool_sems,
):
    steps, depths, rows, islands = sizes
    island = lax.axis_index("island")
    replica = lax.axis_index("replica")
    row = lax.axis_index("shard")
    depth, core = replica // 2, replica % 2
    tokens = x_hbm.shape[1]
    width = xs.shape[3]
    head = t_hbm.shape[2]
    half = weights.shape[3]
    key_scale = (depths * 2 * width) ** (-0.5)
    grad_scale = 1.0 / math.sqrt(tokens * 2 * depths * rows)

    def over_rows(offset):
        return {"shard": (row + offset) % rows}

    def over_depths(offset):
        return {"replica": (depth + offset) % depths * 2 + core}

    sibling = {"replica": depth * 2 + 1 - core}

    def over_islands(offset):
        return {"island": (island + offset) % islands}

    def remote(source, target, send_sem, recv_sem, where):
        return pltpu.make_async_remote_copy(
            src_ref=source, dst_ref=target, send_sem=send_sem, recv_sem=recv_sem,
            device_id=where, device_id_type=MESH,
        )

    barrier = pltpu.get_barrier_semaphore()
    far_rows, far_depths = far_first(rows), far_first(depths)
    near_rows, near_depths = far_rows[::-1], far_depths[::-1]
    outer, inner = far_rows[:3], far_rows[3:]
    greeted = [over_rows(k) for k in far_rows] + [over_depths(k) for k in far_depths]
    greeted += [sibling] + [over_islands(k) for k in range(1, islands)]
    for where in greeted:
        pl.semaphore_signal(barrier, inc=1, device_id=where, device_id_type=MESH)

    def load(k, source):
        return pltpu.make_async_copy(source, state.at[k], state_sems.at[min(k, 1)])

    def loaded(block, sem):
        pltpu.make_async_copy(block, block, sem).wait()

    loads = [load(0, theta_hbm), load(1, momentum_hbm), load(2, first_hbm), load(3, second_hbm)]
    loads[0].start()
    own_tokens = pl.ds(pl.multiple_of(core * tokens, tokens), tokens)

    def x_columns(z, which):
        return pl.ds(pl.multiple_of((z * 2 + which) * width, width), width)

    def x_mine(s, z):
        return pltpu.make_async_copy(
            x_hbm.at[s, :, x_columns(z, core)], xs.at[s, z, own_tokens], x_local.at[s]
        )

    def x_theirs(s, z):
        return remote(
            x_hbm.at[s, :, x_columns(z, 1 - core)], xs.at[s, z, own_tokens],
            x_send.at[0], x_recv.at[s], sibling,
        )

    t_mine = pltpu.make_async_copy(t_hbm, ts.at[:, own_tokens], t_sems.at[0])
    t_theirs = remote(t_hbm, ts.at[:, own_tokens], t_sems.at[1], t_sems.at[2], sibling)
    for z in range(depths):
        x_mine(0, z).start()
    t_mine.start()
    for k in (1, 2, 3):
        loads[k].start()
    for s in range(1, steps):
        for z in range(depths):
            x_mine(s, z).start()

    at_rows, at_depths = 0, rows // 2
    at_a = at_depths + depths // 2
    at_b = at_a + depths - 1
    at_near_a = at_b + depths
    at_near_b = at_near_a + rows
    at_far = at_near_b + depths

    def near_send(s, part, i, where):
        block = weights.at[s, depth * rows + row, part]
        return remote(block, block, send.at[0], recv.at[0, i], where)

    def gather_rows(s, k):
        return near_send(s, 0, at_rows + min(k, rows - k) - 1, over_rows(k))

    def gather_depths(s, k):
        return near_send(s, 1, at_depths + min(k, depths - k) - 1, over_depths(k))

    def received(block, sem):
        remote(block, block, send.at[0], sem, sibling).wait_recv()

    def near_received(s, first, distance, count):
        copies = len({distance, count - distance})
        received(weights.at[s, 0:copies, 0], recv.at[0, first + distance - 1])

    def on_from_row(s, k, targets):
        block = weights.at[s, depth * rows + (row + rows - k) % rows, 0]
        for m in targets:
            remote(block, block, send.at[0], recv.at[0, at_a + m - 1], over_depths(m)).start()

    def on_from_depth(s, k, targets):
        block = weights.at[s, (depth + depths - k) % depths * rows + row, 1]
        for m in targets:
            remote(block, block, send.at[0], recv.at[0, at_b + k], over_rows(m)).start()

    def depth_received(s, k):
        if k > 0:
            received(weights.at[s, 0:rows, 0], recv.at[0, at_a + k - 1])
        received(weights.at[s, 0:rows - 1, 1], recv.at[0, at_b + k])

    def scatter_depths(s, j, k):
        return remote(
            grads.at[s, (depth + k) % depths, (row + j) % rows, 0], near_a.at[s, k - 1, j],
            send.at[1], recv.at[0, at_near_a + j], over_depths(k),
        )

    def scatter_rows(s, j, k):
        return remote(
            grads.at[s, (depth + j) % depths, (row + k) % rows, 1], near_b.at[s, k - 1, j],
            send.at[1], recv.at[0, at_near_b + j], over_rows(k),
        )

    def scatter_far_a(s, k):
        return remote(sum_a.at[s, k], far_a.at[s, k - 1], send.at[1], recv.at[0, at_far], over_rows(k))

    def scatter_far_b(s, k):
        return remote(sum_b.at[s, k], far_b.at[s, k - 1], send.at[1], recv.at[0, at_far + 1], over_depths(k))

    def combine_a(s, j):
        received(near_a.at[s, :, j], recv.at[0, at_near_a + j])
        total = grads[s, depth, (row + j) % rows, 0].astype(F32)
        for k in range(depths - 1):
            total += near_a[s, k, j].astype(F32)
        if j == 0:
            return total
        sum_a[s, j] = total.astype(BF16)
        scatter_far_a(s, j).start()

    def combine_b(s, j):
        received(near_b.at[s, :, j], recv.at[0, at_near_b + j])
        total = grads[s, (depth + j) % depths, row, 1].astype(F32)
        for k in range(rows - 1):
            total += near_b[s, k, j].astype(F32)
        if j == 0:
            return total
        sum_b[s, j] = total.astype(BF16)
        scatter_far_b(s, j).start()

    def gather_start(s, part):
        if part == 0:
            start([gather_rows(s, k) for k in near_rows[:2] + near_rows[6:] + near_rows[2:6]])
        else:
            start([gather_depths(s, k) for k in near_depths])

    def start(copies):
        for copy in copies:
            copy.start()

    def arrive(copies):
        for copy in copies:
            copy.wait_recv()

    near_depth, far_depth = depths > 2, depths // 2
    waits = [(0, 1)] + [(1, 1)] * near_depth + [(0, d) for d in (2, rows // 2, 3) if d < rows // 2 or d == rows // 2 > 1]
    waits = list(dict.fromkeys(waits)) + [(1, far_depth)]

    loads[0].wait()
    weights[0, depth * rows + row] = state[0].astype(BF16)
    pl.semaphore_wait(barrier, len(greeted))
    gather_start(0, 0)
    gather_start(0, 1)

    for s in range(steps):
        on_from_row(s, 0, far_depths)
        on_from_depth(s, 0, far_rows)
        if s == 0:
            for z in range(depths):
                x_theirs(0, z).start()
            t_theirs.start()
        for along, d in waits:
            near_received(s, at_depths if along else at_rows, d, depths if along else rows)
            for k in sorted({d, (depths if along else rows) - d}):
                if along:
                    on_from_depth(s, k, outer)
                else:
                    on_from_row(s, k, far_depths)
        for k in near_depths:
            on_from_depth(s, k, inner)
        if s == 0:
            for later in range(1, steps):
                for z in range(depths):
                    x_theirs(later, z).start()
            t_mine.wait()
            t_theirs.wait_recv()
        loaded(xs.at[s, :, own_tokens], x_local.at[s])
        received(xs.at[s, :, own_tokens], x_recv.at[s])

        def part(p):
            block = part_out.at[s, pl.ds(p * tokens, tokens)]
            return remote(
                block, part_in.at[s, pl.ds(p * tokens, tokens)], part_send.at[0], part_recv.at[s, p], sibling
            )

        for n, k in enumerate([0] + near_depths):
            z = (depth + depths - k) % depths
            depth_received(s, k)
            block = weights[s, pl.ds(z * rows, rows)].reshape(width, head)
            for p in range(2):
                total = jnp.dot(xs[s, z, p * tokens:(p + 1) * tokens], block, preferred_element_type=F32)
                if n > 0:
                    total += part_out[s, p * tokens:(p + 1) * tokens]
                part_out[s, p * tokens:(p + 1) * tokens] = total
                if n == depths - 1:
                    part(p).start()
        arrive([part(0), part(1)])
        projected = (part_out[s] + part_in[s]) * key_scale
        residual = (projected - ts[s].astype(F32)).astype(BF16)

        if s == 0:
            loaded(state.at[1:4], state_sems.at[1])
        for z in far_depths + [0]:
            at = (depth + z) % depths
            gradient = lax.dot_general(
                xs[s, at], residual, (((0,), (0,)), ((), ())), preferred_element_type=F32
            ) * grad_scale
            grads[s, at] = gradient.astype(BF16).reshape(rows, 2, half, head)
            if z > 0:
                start([scatter_depths(s, j, z) for j in outer])
            if z > 0:
                start([scatter_rows(s, z, k) for k in far_rows])
        start([scatter_depths(s, j, z) for j in inner for z in far_depths])
        combine_a(s, far_rows[0])
        start([scatter_rows(s, 0, k) for k in far_rows])
        combine_b(s, far_depths[0])
        start([scatter_depths(s, 0, z) for z in far_depths])
        rest = [(0, j) for j in far_rows[1:3]] + [(1, j) for j in far_depths[1:2]] + [(0, j) for j in far_rows[3:5]]
        rest += [(1, j) for j in far_depths[2:]] + [(0, j) for j in far_rows[5:]]
        for along, j in rest:
            (combine_b if along else combine_a)(s, j)
        totals = {1: combine_b(s, 0), 0: combine_a(s, 0)}

        def update(part_index, gradient):
            parameters = state[0 if s == 0 else 4, part_index]
            first = BETA_ONE * state[2, part_index] + (1.0 - BETA_ONE) * gradient
            second = BETA_TWO * state[3, part_index] + (1.0 - BETA_TWO) * gradient * gradient
            parameters = parameters - INNER_RATE * (
                first / (jnp.sqrt(second) + EPSILON) + DECAY * parameters
            )
            state[2, part_index] = first
            state[3, part_index] = second
            state[4, part_index] = parameters
            if s < steps - 1:
                weights[s + 1, depth * rows + row, part_index] = parameters.astype(BF16)
                gather_start(s + 1, part_index)

        received(far_b.at[s], recv.at[0, at_far + 1])
        for k in range(depths - 1):
            totals[1] += far_b[s, k].astype(F32)
        update(1, totals[1])
        received(far_a.at[s], recv.at[0, at_far])
        for k in range(rows - 1):
            totals[0] += far_a[s, k].astype(F32)
        update(0, totals[0])

    moved = state[0] - state[4]
    pool_out[...] = moved.astype(BF16)

    def pool(k):
        return remote(
            pool_out, pool_in.at[k - 1], pool_sems.at[0], pool_sems.at[1], over_islands(k)
        )

    pools = [pool(k) for k in sorted(range(1, islands), key=lambda k: -min(k % 4, 4 - k % 4))]
    start(pools)

    result[2] = state[2]
    result[3] = state[3]
    def left(block, sem):
        remote(block, block, sem, x_recv.at[0], sibling).wait_send()

    left(xs.at[:, :, own_tokens], x_send.at[0])
    left(ts.at[:, own_tokens], t_sems.at[1])
    left(part_out, part_send.at[0])
    for k in range(2):
        left(weights.at[:, 0:depths * rows - 1], send.at[k])
    received(pool_in, pool_sems.at[1])
    total = moved
    for k in range(islands - 1):
        total += pool_in[k].astype(F32)
    pseudo_grad = total / islands
    momentum_new = OUTER_MOMENTUM * state[1] + pseudo_grad
    result[1] = momentum_new
    result[0] = state[0] - OUTER_RATE * (pseudo_grad + OUTER_MOMENTUM * momentum_new)
    left(pool_in, pool_sems.at[0])


def part_results(result, theta_out, momentum_out, first_out, second_out, sems):
    outs = (theta_out, momentum_out, first_out, second_out)
    copies = [pltpu.make_async_copy(result.at[k], out, sems.at[k]) for k, out in enumerate(outs)]
    for copy in copies:
        copy.start()
    for copy in copies:
        copy.wait()


def per_device(inputs, targets, theta, momentum, first_moment, second_moment):
    steps, tokens, _ = inputs.shape
    block, head = theta.shape
    islands = lax.axis_size("island")
    depths, rows = lax.axis_size("replica") // 2, lax.axis_size("shard")
    half, width = block // 2, rows * block
    split = (2, half, head)
    arrivals = rows // 2 + depths // 2 + depths - 1 + depths + rows + depths + 2
    dma = pltpu.SemaphoreType.DMA
    in_hbm = pl.BlockSpec(memory_space=pltpu.HBM)
    in_vmem = pl.BlockSpec(memory_space=pltpu.VMEM)
    vmem = pltpu.VMEM
    result = pl.pallas_call(
        functools.partial(kernel, (steps, depths, rows, islands)),
        out_shape=pltpu.VMEM((4,) + split, F32),
        in_specs=[in_hbm] * 6,
        out_specs=in_vmem,
        scratch_shapes=[
            vmem((steps, depths, 2 * tokens, width), BF16),
            vmem((steps, 2 * tokens, head), BF16),
            vmem((5,) + split, F32),
            vmem((steps, depths * rows) + split, BF16),
            vmem((steps, 2 * tokens, head), F32),
            vmem((steps, 2 * tokens, head), F32),
            vmem((steps, depths, rows) + split, BF16),
            vmem((steps, depths - 1, rows, half, head), BF16),
            vmem((steps, rows, half, head), BF16),
            vmem((steps, rows - 1, half, head), BF16),
            vmem((steps, rows - 1, depths, half, head), BF16),
            vmem((steps, depths, half, head), BF16),
            vmem((steps, depths - 1, half, head), BF16),
            vmem(split, BF16),
            vmem((islands - 1,) + split, BF16),
            dma((steps,)), dma((1,)), dma((steps,)),
            dma((3,)), dma((2,)),
            dma((1,)), dma((steps, 2)),
            dma((2,)), dma((1, arrivals)),
            dma((2,)),
        ],
        compiler_params=pltpu.CompilerParams(
            collective_id=0, has_side_effects=True, vmem_limit_bytes=60 * 1024 * 1024
        ),
    )(
        inputs, targets, theta.reshape(split), momentum.reshape(split),
        first_moment.reshape(split), second_moment.reshape(split),
    )
    outs = pl.pallas_call(
        part_results,
        out_shape=[jax.ShapeDtypeStruct(split, F32)] * 4,
        in_specs=[in_vmem],
        out_specs=[in_hbm] * 4,
        scratch_shapes=[dma((4,))],
        compiler_params=pltpu.CompilerParams(vmem_limit_bytes=1024 * 1024),
    )(result)
    theta_new, momentum_new, first, second = [out.reshape(block, head) for out in outs]
    return (theta_new, momentum_new, first[None], second[None])


def solution(mesh):
    in_specs = (
        P(None, ("island", "replica", "shard"), None),
        P(None, ("island", "replica", "shard"), None),
        P(("replica", "shard"), None),
        P(("replica", "shard"), None),
        P("island", ("replica", "shard"), None),
        P("island", ("replica", "shard"), None),
    )
    out_specs = (
        P(("replica", "shard"), None),
        P(("replica", "shard"), None),
        P("island", ("replica", "shard"), None),
        P("island", ("replica", "shard"), None),
    )
    return jax.shard_map(
        per_device, mesh=mesh, in_specs=in_specs, out_specs=out_specs, check_vma=False
    )
```
